32 devices in a mesh: parts: 2 (over y), dp: 4 (over z), mp: 2 (over x), rep: 2 (over core).
Axes of the slice: x: 2, y: 2, z: 4, core: 2. Of those that a mesh axis runs over, the one named last changes fastest.
Arguments:
- hidden_in: bfloat16 [64, 256, 1024], P(('parts', 'dp', 'rep')), parts along dimension 0, may hold values from -6 to 6
- doc_lengths: int32 [64], P(('parts', 'dp', 'rep')), parts along dimension 0, may hold values from 32 to 256
- w_qkv: bfloat16 [1024, 3, 1024], P('dp', None, 'mp'), may hold values from -6 to 6
- w_out: bfloat16 [1024, 1024], P('mp', 'dp'), may hold values from -0.1875 to 0.1875
- w_up: bfloat16 [1024, 4096], P('dp', 'mp'), may hold values from -0.1875 to 0.1875
- w_down: bfloat16 [4096, 1024], P('mp', 'dp'), may hold values from -0.09375 to 0.09375
- stored_embed: bfloat16 [2016, 1024], P(('parts', 'dp', 'mp', 'rep')), parts along dimension 0, may hold values from -6 to 6
- doc_labels: int32 [2080, 1], P(('parts', 'dp', 'mp', 'rep')), parts along dimension 0, may hold values from 0 to 3; in each aligned block of 65 rows (0 to 64, 65 to 129, ...) at most 26 rows name the same one
- doc_order: int32 [2080], P(('parts', 'dp', 'mp', 'rep')), parts along dimension 0, may hold values from 0 to 1039, each once
Outputs:
- best: float32 [2080], P(('parts', 'dp', 'mp', 'rep')), parts along dimension 0
The draws below stay inside these ranges and needn't reach their ends.
There are 2 independent parts, one for each index of `parts`. The reference program is written for one: setup_inputs(seed, part) draws one part's arguments, and reference() takes and returns one part's arrays. A program takes and returns all parts, laid end to end along the dimension named above; an argument that names none is the same for every part. Nothing has to cross between parts.
Inputs may be any that keep to these rules, and one draw needn't show every extreme that they name: `doc_labels`: no label appears on more than 26 of the rows of one device. `doc_order`: every rank appears once.
All inputs are finite; a program needn't handle non-finite values.
Results may differ from the reference program's by a relative error of at most 0.005.
Values may be sent and summed in bfloat16 or wider, within the bound.
A program may use at most 64 MiB of HBM per device.

```python
import math
import jax
import jax.numpy as jnp
import numpy as np
from jax import lax

D = 1024
HEADS = 16
HEAD = 64
FF = 4096
SEQ = 256
DOC_DEV = 4
STORE = 63
DOCS = 32
ROWS = 65
STORED = 1008
ALLDOCS = 1040
CLUSTERS = 4
CAP = 26
N_DP = 4
N_MP = 2
N_REP = 2


def draw_w_qkv(key, part):
    first = jax.random.fold_in(key, 0)
    base = jnp.clip(jax.random.normal(first, (D, 3, D), jnp.float32), -6.0, 6.0) * D ** (-0.5)
    return base.astype(jnp.bfloat16)


def with_ends(values, rng, least, top_value):
    extent = values.shape
    index_at = [jax.random.randint(jax.random.fold_in(rng, axis), (), 0, extent[axis]) for axis in range(len(extent))]
    values = values.at[tuple(index_at)].set(least)
    longest = extent.index(max(extent))
    index_at[longest] = (index_at[longest] + 1) % extent[longest]
    return values.at[tuple(index_at)].set(top_value)


def level_of(rng, shape, pieces, least, high):
    gain, own = 1.0, jax.random.fold_in(rng, 6)
    for dim, blocks in pieces:
        heights = jnp.exp(jax.random.uniform(jax.random.fold_in(own, dim), (blocks,), jnp.float32, least / len(pieces), high / len(pieces)))
        gain = gain * jnp.repeat(heights, shape[dim] // blocks).reshape([-1 if axis == dim else 1 for axis in range(len(shape))])
    return gain


def deal_out(own_key, own, number, rows, number_of, top, bound, lean):
    ranking = jax.random.permutation(own_key, number_of)
    crowded, common = portions_of(number_of, rows * top, bound, lean, True), portions_of(number_of, rows * top, bound, lean, False)
    places = jnp.arange(number_of)

    def named(lengths, rotation):
        used = int((lengths > 0).sum())
        fixed = max(1, used // 4)
        shifted = fixed + (places - fixed + rotation * (used - fixed)) % max(1, number_of - fixed)
        return jnp.zeros((number_of,), jnp.int32).at[ranking[jnp.where(places < fixed, places, shifted)]].set(jnp.asarray(lengths, jnp.int32))

    lengths = jnp.where(number % 4 == 0, named(crowded, number // 4), named(common, number - number // 4 - 1))
    mixed = jax.random.permutation(jax.random.fold_in(own, 3), number_of)
    donor, sink = mixed[0:number_of // 2 * 2:2], mixed[1:number_of // 2 * 2:2]
    slack = jnp.minimum(lengths[donor] - 1, bound - lengths[sink]) // 2
    slack = jnp.where((donor == ranking[0]) | (sink == ranking[0]) | (lengths[sink] == 0), 0, jnp.maximum(slack, 0))
    shifted = jax.random.randint(jax.random.fold_in(own, 4), (number_of // 2,), 0, 1 << 20) % (slack + 1)
    lengths = lengths.at[donor].add(-shifted).at[sink].add(shifted)
    items = jnp.searchsorted(jnp.cumsum(lengths), jnp.arange(rows * top), side="right").astype(jnp.int32)
    listing = items.reshape(top, rows).T
    listing = listing[jax.random.permutation(jax.random.fold_in(own, 1), rows)]
    rotation = jax.random.randint(jax.random.fold_in(own, 2), (rows, 1), 0, top)
    return jnp.take_along_axis(listing, (jnp.arange(top)[None, :] + rotation) % top, axis=1)


def portions_of(amount, total, limit, slope, full):
    portions = [(1 << 20) // math.isqrt(standing ** slope) + 1 for standing in range(1, amount + 1)]
    largest = limit if full else min(limit, max(-(-total // amount), total * portions[0] // sum(portions)))
    least = 1 if total - largest >= amount - 1 else 0
    holding, surplus = [largest] + [least] * (amount - 1), total - largest - least * (amount - 1)
    while surplus > 0:
        candidates = [i for i in range(1, amount) if holding[i] < largest] or [i for i in range(1, amount) if holding[i] < limit]
        pool, left = sum([portions[i] for i in candidates]), surplus
        for i in candidates:
            more = min(limit - holding[i], max(1, left * portions[i] // pool), surplus)
            holding[i] = holding[i] + more
            surplus = surplus - more
    return np.array(holding)


def bell_draw(own_key, extent, scale, most, cuts=(), kind=jnp.bfloat16):
    array = scale * jax.random.normal(own_key, extent, jnp.float32)
    if cuts:
        array = array * level_of(own_key, extent, cuts, -0.22, 0.18)
    return jnp.clip(array, -most, most).astype(kind)


def setup_inputs(seed: int = 0, part: int = 0) -> dict:
    seeds = jax.random.split(jax.random.key(seed), 10)
    part_splits = jax.random.split(jax.random.fold_in(seeds[9], part), 10)
    hidden_in = bell_draw(part_splits[0], (DOCS, SEQ, D), 1.0, 6.0, ((0, 8),))
    doc_lengths = with_ends(jax.random.randint(part_splits[1], (DOCS,), SEQ // 8, SEQ + 1), jax.random.fold_in(part_splits[1], 1), SEQ // 8, SEQ).astype(jnp.int32)
    w_qkv = draw_w_qkv(jax.random.fold_in(seeds[9], 71), part)
    w_out = bell_draw(seeds[3], (D, D), D ** -0.5, 0.1875, ((0, 2), (1, 4)))
    w_up = bell_draw(seeds[4], (D, FF), D ** -0.5, 0.1875, ((0, 4), (1, 2)))
    w_down = bell_draw(seeds[5], (FF, D), FF ** -0.5, 0.09375, ((0, 2), (1, 4)))
    stored_embed = bell_draw(part_splits[6], (STORED, D), 1.0, 6.0, ((0, 16),))
    doc_labels_keys = jax.random.split(jax.random.fold_in(part_splits[7], 1), ALLDOCS // ROWS)
    doc_labels_turns = jax.random.permutation(jax.random.fold_in(part_splits[7], 3), ALLDOCS // ROWS)
    doc_labels = jax.vmap(lambda own, number: deal_out(jax.random.fold_in(part_splits[7], 2), own, number, ROWS, CLUSTERS, 1, CAP, 2))(doc_labels_keys, doc_labels_turns).reshape((ALLDOCS, 1))
    doc_order = jax.random.permutation(part_splits[8], ALLDOCS).astype(jnp.int32)
    return {"hidden_in": hidden_in, "doc_lengths": doc_lengths, "w_qkv": w_qkv, "w_out": w_out, "w_up": w_up, "w_down": w_down, "stored_embed": stored_embed, "doc_labels": doc_labels, "doc_order": doc_order}


def normalize(values):
    centred = values - lax.optimization_barrier(jnp.mean(values, axis=-1, keepdims=True))
    spread = lax.optimization_barrier(jnp.mean(centred * centred, axis=-1, keepdims=True))
    return centred * lax.rsqrt(spread + 1e-05)

def unit_rows(values):
    return (values * lax.rsqrt(lax.optimization_barrier(jnp.sum(values * values, axis=-1, keepdims=True)) + 1e-06)).astype(jnp.bfloat16)

def encode_one(hidden, length, w_qkv, w_out, w_up, w_down):
    residual = hidden.astype(jnp.float32)
    normed = normalize(residual).astype(jnp.bfloat16)
    projected = jnp.einsum('sd,dte->ste', normed.astype(jnp.float32), w_qkv.astype(jnp.float32)).astype(jnp.bfloat16)
    stacked = projected.reshape(SEQ, 3, HEADS, HEAD)
    queries = stacked[:, 0].astype(jnp.float32)
    key_heads = stacked[:, 1].astype(jnp.float32)
    values = stacked[:, 2].astype(jnp.float32)
    scores = jnp.einsum('qhe,khe->hqk', queries, key_heads) * HEAD ** (-0.5)
    positions = jnp.arange(SEQ, dtype=jnp.int32)
    key_valid = positions < length
    scores = jnp.where(key_valid[None, None, :], scores, -jnp.inf)
    attention = jax.nn.softmax(scores, axis=-1).astype(jnp.bfloat16)
    context = jnp.einsum('hqk,khe->qhe', attention.astype(jnp.float32), values).astype(jnp.bfloat16)
    context = context.reshape(SEQ, N_MP, D // N_MP).astype(jnp.float32)
    grouped = jnp.einsum('sgf,gfd->gsd', context, w_out.reshape(N_MP, D // N_MP, D).astype(jnp.float32))
    rounded = lax.optimization_barrier(grouped.astype(jnp.bfloat16))
    residual = residual + lax.optimization_barrier(jnp.sum(rounded.astype(jnp.float32), axis=0))
    hidden_normed = normalize(residual).astype(jnp.bfloat16)
    activated = jax.nn.gelu(jnp.dot(hidden_normed, w_up, preferred_element_type=jnp.float32), approximate=False).astype(jnp.bfloat16)
    mlp_out = jnp.dot(activated, w_down, preferred_element_type=jnp.float32)
    valid = key_valid.astype(jnp.float32)
    return lax.optimization_barrier(jnp.sum(valid[:, None] * (residual + mlp_out), axis=0)) / length.astype(jnp.float32)

def reference(hidden_in, doc_lengths, w_qkv, w_out, w_up, w_down, stored_embed, doc_labels, doc_order):

    def encode_item(item):
        return encode_one(item[0], item[1], w_qkv, w_out, w_up, w_down)
    pooled = lax.map(encode_item, (hidden_in, doc_lengths))
    new_units = unit_rows(pooled)
    new_count = DOC_DEV // N_MP
    arranged = new_units.reshape(N_DP, N_REP, N_MP, new_count, D).transpose(0, 2, 1, 3, 4)
    stored_units = unit_rows(stored_embed.astype(jnp.float32)).reshape(N_DP, N_MP, N_REP, STORE, D)
    all_units = jnp.concatenate([arranged, stored_units], axis=3).reshape(-1, D)
    labels_flat = doc_labels[:, 0]

    def best_block(item):
        units, labels_here, order_here = item
        similar = jnp.dot(units, all_units.T, preferred_element_type=jnp.float32)
        earlier = (labels_flat[None, :] == labels_here[:, None]) & (doc_order[None, :] < order_here[:, None])
        largest = lax.optimization_barrier(jnp.max(jnp.where(earlier, similar, -2.0), axis=1))
        return jnp.where(largest < -1.5, 0.0, largest)
    best = lax.map(best_block, (all_units.reshape(-1, ROWS, D), labels_flat.reshape(-1, ROWS), doc_order.reshape(-1, ROWS)))
    return best.reshape(-1)
```

```python
import functools

import jax
import jax.numpy as jnp
from jax import lax
from jax.experimental import pallas as pl
from jax.experimental.pallas import tpu as pltpu
from jax.sharding import PartitionSpec as P

HEAD = 64
LANES = 128
MESH = pl.DeviceIdType.MESH


def unit_rows(values):
    return (values * lax.rsqrt(jnp.sum(values * values, axis=-1, keepdims=True) + 1e-06)).astype(
        jnp.bfloat16
    )


def normed_rows(values):
    centred = values - jnp.mean(values, axis=-1, keepdims=True)
    spread = jnp.mean(centred * centred, axis=-1, keepdims=True)
    return (centred * lax.rsqrt(spread + 1e-05)).astype(jnp.bfloat16)


def encode_kernel(
    n, mps, splits, len_ref, hid_ref, wq_ref, wo_ref, wu_ref, act_ref, res_ref,
    q_buf, o_buf, u_buf, c_buf, proj, z_send, z_recv, c_send, c_recv, x_send, x_recv, y_send, y_recv,
):
    me, my_mp = lax.axis_index("dp"), lax.axis_index("mp")
    part, rep = lax.axis_index("parts"), lax.axis_index("rep")
    docs, seq, _ = hid_ref.shape
    heads_wide = c_buf.shape[3]
    depth = wq_ref.shape[0]
    out_rows = wo_ref.shape[0]

    def piece(which, source, p, r):
        number = splits[which]
        group = p * 2 + r if number == 4 else p
        if which == 1:
            rows = out_rows // number
            return o_buf.at[my_mp, source, pl.ds(pl.multiple_of(group * rows, 16), rows), :]
        buf = q_buf if which == 0 else u_buf
        wide = buf.shape[1] // number
        return buf.at[
            pl.ds(pl.multiple_of(source * depth, 16), depth),
            pl.ds(pl.multiple_of(group * wide, LANES), wide),
        ]

    def copy_of(which, source, p, r, send, recv, device):
        ref = piece(which, source, p, r)
        return pltpu.make_async_remote_copy(
            src_ref=ref, dst_ref=ref, send_sem=z_send.at[which, source, send],
            recv_sem=z_recv.at[which, source, recv], device_id=device, device_id_type=MESH,
        )

    def right(which, source):
        return copy_of(which, source, part, rep, 0, 0, {"dp": me + 1})

    def left(which, source):
        return copy_of(which, source, part, rep, 4, 0, {"dp": me - 1})

    def across(which, source, p):
        return copy_of(which, source, p, rep, 1, 1, {"parts": 1 - part})

    def beside(which, source, r):
        return copy_of(which, source, part, r, 2, 2, {"rep": 1 - rep})

    def beside_late(which, source, p, r):
        return copy_of(which, source, p, r, 3, 3, {"rep": 1 - rep})

    def own(which):
        @pl.when(me < n - 1)
        def _():
            right(which, me).start()

        @pl.when(me > 0)
        def _():
            left(which, me).start()

    def on_z(which, source, rightward):
        way = right if rightward else left
        way(which, source).wait_recv()

        @pl.when(me < n - 1 if rightward else me > 0)
        def _():
            way(which, source).start()

        across(which, source, part).start()
        if splits[which] == 4:
            beside(which, source, rep).start()

    def on_y(which, source):
        across(which, source, 1 - part).wait_recv()
        if splits[which] == 4:
            beside_late(which, source, 1 - part, rep).start()

    def both(step, fn):
        @pl.when(step <= me)
        def _():
            fn(me - step, True)

        @pl.when(me + step <= n - 1)
        def _():
            fn(me + step, False)

    def steps(which, lo, hi):
        def body(step, carry):
            both(step, lambda source, way: on_z(which, source, way))

            @pl.when(step > 1)
            def _():
                both(step - 1, lambda source, way: on_y(which, source))

            return carry

        lax.fori_loop(lo, hi, body, 0)

    def finish(which):
        both(n - 1, lambda source, way: on_y(which, source))
        if splits[which] == 4:

            def body(step, carry):
                def take(source, way):
                    beside(which, source, 1 - rep).wait_recv()
                    beside_late(which, source, 1 - part, 1 - rep).wait_recv()

                both(step, take)
                return carry

            lax.fori_loop(1, n, body, 0)

    def sent(which):
        @pl.when(me < n - 1)
        def _():
            right(which, me).wait_send()

        @pl.when(me > 0)
        def _():
            left(which, me).wait_send()

        def body(step, carry):
            def drop(source, way):
                @pl.when(me < n - 1 if way else me > 0)
                def _():
                    (right if way else left)(which, source).wait_send()

                across(which, source, part).wait_send()
                if splits[which] == 4:
                    beside(which, source, rep).wait_send()
                    beside_late(which, source, 1 - part, rep).wait_send()

            both(step, drop)
            return carry

        lax.fori_loop(1, n, body, 0)

    def other(k):
        return lax.rem(my_mp + k, mps)

    def context_copy(owner, k, doc):
        ref = c_buf.at[owner, doc]
        return pltpu.make_async_remote_copy(
            src_ref=ref, dst_ref=ref, send_sem=c_send.at[k, doc], recv_sem=c_recv.at[owner, doc],
            device_id={"mp": other(k)}, device_id_type=MESH,
        )

    half = out_rows // 2

    def out_half(owner, r):
        return o_buf.at[owner, :, pl.ds(pl.multiple_of(r * half, 16), half), :]

    def out_copy(owner, k):
        ref = out_half(owner, rep)
        return pltpu.make_async_remote_copy(
            src_ref=ref, dst_ref=ref, send_sem=x_send.at[k], recv_sem=x_recv.at[owner],
            device_id={"mp": other(k)}, device_id_type=MESH,
        )

    def out_beside(owner, r):
        ref = out_half(owner, r)
        return pltpu.make_async_remote_copy(
            src_ref=ref, dst_ref=ref, send_sem=y_send.at[owner], recv_sem=y_recv.at[owner],
            device_id={"rep": 1 - rep}, device_id_type=MESH,
        )

    q_buf[pl.ds(pl.multiple_of(me * depth, 16), depth), :] = wq_ref[...]
    o_buf[my_mp, me] = wo_ref[...]
    u_buf[pl.ds(pl.multiple_of(me * depth, 16), depth), :] = wu_ref[...]

    barrier = pltpu.get_barrier_semaphore()

    @pl.when(me < n - 1)
    def _():
        pl.semaphore_signal(barrier, inc=1, device_id={"dp": me + 1}, device_id_type=MESH)

    @pl.when(me > 0)
    def _():
        pl.semaphore_signal(barrier, inc=1, device_id={"dp": me - 1}, device_id_type=MESH)

    pl.semaphore_signal(barrier, inc=1, device_id={"parts": 1 - part}, device_id_type=MESH)
    pl.semaphore_signal(barrier, inc=1, device_id={"rep": 1 - rep}, device_id_type=MESH)
    for k in range(1, mps):
        pl.semaphore_signal(barrier, inc=1, device_id={"mp": other(k)}, device_id_type=MESH)

    inner = (me > 0) & (me < n - 1)

    @pl.when(inner)
    def _():
        pl.semaphore_wait(barrier, 3 + mps)

    @pl.when(jnp.logical_not(inner))
    def _():
        pl.semaphore_wait(barrier, 2 + mps)

    own(0)
    own(1)
    steps(0, 1, n - 1)
    own(2)
    steps(0, n - 1, n)
    finish(0)

    lanes = lax.broadcasted_iota(jnp.int32, (1, LANES), 1) < HEAD
    keys_at = lax.broadcasted_iota(jnp.int32, (1, seq), 1)
    cuts = [1 + (n - 1) * k // 3 for k in range(4)]

    def attend(doc, carry):
        normed = normed_rows(hid_ref[doc].astype(jnp.float32))
        proj[...] = jnp.dot(normed, q_buf[...], preferred_element_type=jnp.float32).astype(jnp.bfloat16)
        visible = keys_at < len_ref[doc]

        for pair in range(heads_wide // LANES):
            queries = proj[:, pair * LANES:(pair + 1) * LANES]
            keys = proj[:, heads_wide + pair * LANES:heads_wide + (pair + 1) * LANES]
            values = proj[:, 2 * heads_wide + pair * LANES:2 * heads_wide + (pair + 1) * LANES]
            queries = queries * jnp.asarray(HEAD ** (-0.5), jnp.bfloat16)
            blank = jnp.zeros_like(queries)
            made = []
            for mine in (lanes, jnp.logical_not(lanes)):
                scores = lax.dot_general(
                    jnp.where(mine, queries, blank), keys, (((1,), (1,)), ((), ())),
                    preferred_element_type=jnp.float32,
                )
                scores = jnp.where(visible, scores, -jnp.inf)
                weights = jnp.exp(scores - jnp.max(scores, axis=1, keepdims=True))
                total = jnp.sum(weights, axis=1, keepdims=True)
                weights = (weights / total).astype(jnp.bfloat16)
                made.append(jnp.dot(weights, values, preferred_element_type=jnp.float32))
            context = jnp.where(lanes, made[0], made[1]).astype(jnp.bfloat16)
            c_buf[my_mp, doc, :, pair * LANES:(pair + 1) * LANES] = context

        for k in range(1, mps):
            context_copy(my_mp, k, doc).start()

        @pl.when(doc == 0)
        def _():
            steps(1, 1, n)
            finish(1)
            for k in range(1, mps):
                out_copy(my_mp, k).start()

        for k in range(3):
            @pl.when(doc == min(k + 1, docs - 1))
            def _():
                steps(2, cuts[k], cuts[k + 1])

        return carry

    lax.fori_loop(0, docs, attend, 0)
    for k in range(1, mps):
        out_copy(other(k), k).wait_recv()
        out_beside(other(k), rep).start()
    finish(2)
    for k in range(1, mps):
        out_beside(other(k), 1 - rep).wait_recv()

    def feed(doc, carry):
        for k in range(1, mps):
            context_copy(other(k), k, doc).wait_recv()
        residual = hid_ref[doc].astype(jnp.float32)
        for owner in range(mps):
            context = c_buf[owner, doc]
            product = jnp.concatenate(
                [jnp.dot(context, o_buf[owner, j], preferred_element_type=jnp.float32) for j in range(n)], axis=1
            )
            residual = residual + product.astype(jnp.bfloat16).astype(jnp.float32)
        valid = lax.broadcasted_iota(jnp.int32, (seq, 1), 0) < len_ref[doc]
        res_ref[doc] = jnp.sum(jnp.where(valid, residual, 0.0), axis=0, keepdims=True)
        normed = normed_rows(residual)
        wide = u_buf.shape[1]
        block = wide // 4
        for k in range(4):
            hidden = jnp.dot(normed, u_buf[:, k * block:(k + 1) * block], preferred_element_type=jnp.float32)
            hidden = 0.5 * hidden * (1.0 + lax.erf(hidden * (0.5 ** 0.5)))
            hidden = hidden.astype(jnp.bfloat16).astype(jnp.float32)
            act_ref[doc, :, k * block:(k + 1) * block] = jnp.sum(
                jnp.where(valid, hidden, 0.0), axis=0, keepdims=True
            )
        return carry

    lax.fori_loop(0, docs, feed, 0)

    for which in range(3):
        sent(which)

    def unsent(doc, carry):
        for k in range(1, mps):
            context_copy(my_mp, k, doc).wait_send()
        return carry

    lax.fori_loop(0, docs, unsent, 0)
    for k in range(1, mps):
        out_copy(my_mp, k).wait_send()
        out_beside(other(k), rep).wait_send()


def encode(lengths, hidden, w_qkv, w_out, w_up):
    n, mps = lax.axis_size("dp"), lax.axis_size("mp")
    docs, seq, width = hidden.shape
    splits = tuple(
        4 if extent % (4 * unit) == 0 else 2
        for extent, unit in ((w_qkv.shape[1], LANES), (w_out.shape[0], 16), (w_up.shape[1], LANES))
    )
    heads_wide = w_qkv.shape[1] // 3
    whole = pl.BlockSpec(memory_space=pltpu.VMEM)
    dma = pltpu.SemaphoreType.DMA
    return pl.pallas_call(
        functools.partial(encode_kernel, n, mps, splits),
        out_shape=(
            jax.ShapeDtypeStruct((docs, 1, w_up.shape[1]), jnp.float32),
            jax.ShapeDtypeStruct((docs, 1, width), jnp.float32),
        ),
        in_specs=[pl.BlockSpec(memory_space=pltpu.SMEM)] + [whole] * 4,
        out_specs=(whole, whole),
        scratch_shapes=[
            pltpu.VMEM((width, w_qkv.shape[1]), jnp.bfloat16),
            pltpu.VMEM((mps, n) + w_out.shape, jnp.bfloat16),
            pltpu.VMEM((width, w_up.shape[1]), jnp.bfloat16),
            pltpu.VMEM((mps, docs, seq, heads_wide), jnp.bfloat16),
            pltpu.VMEM((seq, w_qkv.shape[1]), jnp.bfloat16),
            dma((3, n, 5)),
            dma((3, n, 4)),
            dma((mps, docs)),
            dma((mps, docs)),
            dma((mps,)),
            dma((mps,)),
            dma((mps,)),
            dma((mps,)),
        ],
        compiler_params=pltpu.CompilerParams(
            collective_id=0, has_side_effects=True, vmem_limit_bytes=52 * 1024 * 1024
        ),
        cost_estimate=pl.CostEstimate(flops=12 * 10**9, bytes_accessed=10**8, transcendentals=10**6),
    )(lengths, hidden, w_qkv, w_out, w_up)


def pool_kernel(n, mps, reps, act_ref, res_ref, w_ref, out_ref, a_buf, r_buf, a_send, a_recv, r_send, r_recv, p_send, p_recv):
    me, my_mp, rep = lax.axis_index("dp"), lax.axis_index("mp"), lax.axis_index("rep")
    count = n * mps * reps
    place = (me * mps + my_mp) * reps + rep

    def at(number):
        return {"dp": number // (mps * reps), "mp": number // reps % mps, "rep": number % reps}

    barrier = pltpu.get_barrier_semaphore()

    def greet(k, carry):
        pl.semaphore_signal(barrier, inc=1, device_id=at(lax.rem(place + k, count)), device_id_type=MESH)
        return carry

    lax.fori_loop(1, count, greet, 0)
    pl.semaphore_wait(barrier, count - 1)

    def act_copy(source, target):
        return pltpu.make_async_remote_copy(
            src_ref=act_ref, dst_ref=a_buf.at[source], send_sem=a_send.at[target], recv_sem=a_recv.at[source],
            device_id={"dp": target}, device_id_type=MESH,
        )

    def res_copy(source, target):
        return pltpu.make_async_remote_copy(
            src_ref=res_ref.at[target], dst_ref=r_buf.at[source], send_sem=r_send.at[target],
            recv_sem=r_recv.at[source], device_id={"dp": target}, device_id_type=MESH,
        )

    def give(k, carry):
        target = lax.rem(me + k, n)
        act_copy(me, target).start()
        res_copy(me, target).start()
        return carry

    lax.fori_loop(1, n, give, 0)
    a_buf[me] = act_ref[...]
    r_buf[me] = res_ref[me]

    def take(k, carry):
        source = lax.rem(me + k, n)
        act_copy(source, source).wait()
        res_copy(source, source).wait()
        return carry

    lax.fori_loop(1, n, take, 0)
    acts = jnp.concatenate([a_buf[j] for j in range(n)], axis=0)
    high = acts.astype(jnp.bfloat16)
    low = (acts - high.astype(jnp.float32)).astype(jnp.bfloat16)
    part = jnp.dot(high, w_ref[...], preferred_element_type=jnp.float32)
    part = part + jnp.dot(low, w_ref[...], preferred_element_type=jnp.float32)
    rest = jnp.concatenate([r_buf[j] for j in range(n)], axis=0)
    out_ref[place] = part + jnp.where(my_mp == 0, 1.0, 0.0) * rest

    def part_copy(source, target):
        return pltpu.make_async_remote_copy(
            src_ref=out_ref.at[source], dst_ref=out_ref.at[source], send_sem=p_send.at[target],
            recv_sem=p_recv.at[source], device_id=at(target), device_id_type=MESH,
        )

    def share(k, carry):
        part_copy(place, lax.rem(place + k, count)).start()
        return carry

    lax.fori_loop(1, count, share, 0)

    def collect(k, carry):
        source = lax.rem(place + k, count)
        part_copy(source, source).wait()
        return carry

    lax.fori_loop(1, count, collect, 0)


def pool(acts, rest, w_down):
    n, mps, reps = lax.axis_size("dp"), lax.axis_size("mp"), lax.axis_size("rep")
    docs = acts.shape[0]
    count = n * mps * reps
    whole = pl.BlockSpec(memory_space=pltpu.VMEM)
    dma = pltpu.SemaphoreType.DMA
    return pl.pallas_call(
        functools.partial(pool_kernel, n, mps, reps),
        out_shape=jax.ShapeDtypeStruct((count, n * docs, w_down.shape[1]), jnp.float32),
        in_specs=[whole] * 3,
        out_specs=whole,
        scratch_shapes=[
            pltpu.VMEM((n,) + acts.shape, jnp.float32),
            pltpu.VMEM(rest.shape, jnp.float32),
            dma((n,)), dma((n,)), dma((n,)), dma((n,)), dma((count,)), dma((count,)),
        ],
        compiler_params=pltpu.CompilerParams(
            collective_id=1, has_side_effects=True, vmem_limit_bytes=52 * 1024 * 1024
        ),
    )(acts, rest, w_down)


def shards(hidden_in, doc_lengths, w_qkv, w_out, w_up, w_down, stored_embed, doc_labels, doc_order):
    n, mps, reps = lax.axis_size("dp"), lax.axis_size("mp"), lax.axis_size("rep")
    docs, _, width = hidden_in.shape
    place = (lax.axis_index("dp") * mps + lax.axis_index("mp")) * reps + lax.axis_index("rep")
    blocks = n * mps * reps
    rows = doc_order.shape[0]
    new_count = docs // mps
    ranks = blocks * rows

    stored_units = unit_rows(stored_embed.astype(jnp.float32))
    labels = doc_labels[:, 0]
    own_key = labels * ranks + doc_order
    spare = -stored_units.shape[0] % 16
    all_stored = lax.all_gather(
        jnp.pad(stored_units, ((0, spare), (0, 0))), ("dp", "mp", "rep"), axis=0, tiled=True
    )
    keys = lax.all_gather(own_key, ("dp", "mp", "rep"), axis=0, tiled=False)
    stored_keys = jnp.pad(keys[:, new_count:], ((0, 0), (0, spare)), constant_values=-1)

    acts, rest = encode(doc_lengths, hidden_in, w_qkv.reshape(w_qkv.shape[0], -1), w_out, w_up)
    scale = 1.0 / doc_lengths[:, None].astype(jnp.float32)
    acts = acts[:, 0] * scale
    rest = (rest[:, 0] * scale).reshape(docs, n, width // n).transpose(1, 0, 2)
    parts = pool(acts, rest, w_down)
    pooled = jnp.sum(parts.reshape(n, mps, reps, n, docs, width // n), axis=1)
    pooled = pooled.transpose(2, 1, 3, 0, 4).reshape(n, reps, mps, new_count, width)
    new_units = unit_rows(pooled).transpose(0, 2, 1, 3, 4).reshape(blocks * new_count, width)
    own_new = lax.dynamic_slice_in_dim(new_units, place * new_count, new_count, 0)
    own_rows = jnp.concatenate([own_new, stored_units], axis=0)

    def best_of(units, unit_keys):
        similar = lax.dot_general(
            own_rows, units, (((1,), (1,)), ((), ())), preferred_element_type=jnp.float32
        )
        unit_keys = unit_keys.reshape(1, -1)
        earlier = (unit_keys < own_key[:, None]) & (unit_keys >= (labels * ranks)[:, None])
        return jnp.max(jnp.where(earlier, similar, -2.0), axis=1)

    largest = jnp.maximum(best_of(all_stored, stored_keys), best_of(new_units, keys[:, :new_count]))
    return jnp.where(largest < -1.5, 0.0, largest)


def solution(mesh):
    placed = (
        P(("parts", "dp", "rep"), None, None),
        P(("parts", "dp", "rep")),
        P("dp", None, "mp"),
        P("mp", "dp"),
        P("dp", "mp"),
        P("mp", "dp"),
        P(("parts", "dp", "mp", "rep"), None),
        P(("parts", "dp", "mp", "rep"), None),
        P(("parts", "dp", "mp", "rep")),
    )
    return jax.shard_map(
        shards,
        mesh=mesh,
        in_specs=placed,
        out_specs=P(("parts", "dp", "mp", "rep")),
        check_vma=False,
    )
```

```python
import functools

import jax
import jax.numpy as jnp
from jax import lax
from jax.experimental import pallas as pl
from jax.experimental.pallas import tpu as pltpu
from jax.sharding import PartitionSpec as P

HEAD = 64
LANES = 128
MESH = pl.DeviceIdType.MESH


def unit_rows(values):
    return (values * lax.rsqrt(jnp.sum(values * values, axis=-1, keepdims=True) + 1e-06)).astype(
        jnp.bfloat16
    )


def normed_rows(values):
    centred = values - jnp.mean(values, axis=-1, keepdims=True)
    spread = jnp.mean(centred * centred, axis=-1, keepdims=True)
    return (centred * lax.rsqrt(spread + 1e-05)).astype(jnp.bfloat16)


def encode_kernel(
    n, mps, splits, len_ref, hid_ref, wq_ref, wo_ref, wu_ref, act_ref, res_ref,
    q_buf, o_buf, u_buf, c_buf, proj, z_send, z_recv, c_send, c_recv, x_send, x_recv, y_send, y_recv,
):
    me, my_mp = lax.axis_index("dp"), lax.axis_index("mp")
    part, rep = lax.axis_index("parts"), lax.axis_index("rep")
    docs, seq, _ = hid_ref.shape
    heads_wide = c_buf.shape[3]
    depth = wq_ref.shape[0]
    out_rows = wo_ref.shape[0]

    def piece(which, source, p, r):
        number = splits[which]
        group = p * 2 + r if number == 4 else p
        if which == 1:
            rows = out_rows // number
            return o_buf.at[my_mp, source, pl.ds(pl.multiple_of(group * rows, 16), rows), :]
        buf = q_buf if which == 0 else u_buf
        wide = buf.shape[1] // number
        return buf.at[
            pl.ds(pl.multiple_of(source * depth, 16), depth),
            pl.ds(pl.multiple_of(group * wide, LANES), wide),
        ]

    def copy_of(which, source, p, r, send, recv, device):
        ref = piece(which, source, p, r)
        return pltpu.make_async_remote_copy(
            src_ref=ref, dst_ref=ref, send_sem=z_send.at[which, source, send],
            recv_sem=z_recv.at[which, source, recv], device_id=device, device_id_type=MESH,
        )

    def right(which, source):
        return copy_of(which, source, part, rep, 0, 0, {"dp": me + 1})

    def left(which, source):
        return copy_of(which, source, part, rep, 4, 0, {"dp": me - 1})

    def across(which, source, p):
        return copy_of(which, source, p, rep, 1, 1, {"parts": 1 - part})

    def beside(which, source, r):
        return copy_of(which, source, part, r, 2, 2, {"rep": 1 - rep})

    def beside_late(which, source, p, r):
        return copy_of(which, source, p, r, 3, 3, {"rep": 1 - rep})

    def own(which):
        @pl.when(me < n - 1)
        def _():
            right(which, me).start()

        @pl.when(me > 0)
        def _():
            left(which, me).start()

    def on_z(which, source, rightward):
        way = right if rightward else left
        way(which, source).wait_recv()

        @pl.when(me < n - 1 if rightward else me > 0)
        def _():
            way(which, source).start()

        across(which, source, part).start()
        if splits[which] == 4:
            beside(which, source, rep).start()

    def on_y(which, source):
        across(which, source, 1 - part).wait_recv()
        if splits[which] == 4:
            beside_late(which, source, 1 - part, rep).start()

    def both(step, fn):
        @pl.when(step <= me)
        def _():
            fn(me - step, True)

        @pl.when(me + step <= n - 1)
        def _():
            fn(me + step, False)

    def steps(which, lo, hi):
        def body(step, carry):
            both(step, lambda source, way: on_z(which, source, way))

            @pl.when(step > 1)
            def _():
                both(step - 1, lambda source, way: on_y(which, source))

            return carry

        lax.fori_loop(lo, hi, body, 0)

    def finish(which):
        both(n - 1, lambda source, way: on_y(which, source))
        if splits[which] == 4:

            def body(step, carry):
                def take(source, way):
                    beside(which, source, 1 - rep).wait_recv()
                    beside_late(which, source, 1 - part, 1 - rep).wait_recv()

                both(step, take)
                return carry

            lax.fori_loop(1, n, body, 0)

    def sent(which):
        @pl.when(me < n - 1)
        def _():
            right(which, me).wait_send()

        @pl.when(me > 0)
        def _():
            left(which, me).wait_send()

        def body(step, carry):
            def drop(source, way):
                @pl.when(me < n - 1 if way else me > 0)
                def _():
                    (right if way else left)(which, source).wait_send()

                across(which, source, part).wait_send()
                if splits[which] == 4:
                    beside(which, source, rep).wait_send()
                    beside_late(which, source, 1 - part, rep).wait_send()

            both(step, drop)
            return carry

        lax.fori_loop(1, n, body, 0)

    def other(k):
        return lax.rem(my_mp + k, mps)

    def context_copy(owner, k, doc):
        ref = c_buf.at[owner, doc]
        return pltpu.make_async_remote_copy(
            src_ref=ref, dst_ref=ref, send_sem=c_send.at[k, doc], recv_sem=c_recv.at[owner, doc],
            device_id={"mp": other(k)}, device_id_type=MESH,
        )

    half = out_rows // 2

    def out_half(owner, r):
        return o_buf.at[owner, :, pl.ds(pl.multiple_of(r * half, 16), half), :]

    def out_copy(owner, k):
        ref = out_half(owner, rep)
        return pltpu.make_async_remote_copy(
            src_ref=ref, dst_ref=ref, send_sem=x_send.at[k], recv_sem=x_recv.at[owner],
            device_id={"mp": other(k)}, device_id_type=MESH,
        )

    def out_beside(owner, r):
        ref = out_half(owner, r)
        return pltpu.make_async_remote_copy(
            src_ref=ref, dst_ref=ref, send_sem=y_send.at[owner], recv_sem=y_recv.at[owner],
            device_id={"rep": 1 - rep}, device_id_type=MESH,
        )

    q_buf[pl.ds(pl.multiple_of(me * depth, 16), depth), :] = wq_ref[...]
    o_buf[my_mp, me] = wo_ref[...]
    u_buf[pl.ds(pl.multiple_of(me * depth, 16), depth), :] = wu_ref[...]

    barrier = pltpu.get_barrier_semaphore()

    @pl.when(me < n - 1)
    def _():
        pl.semaphore_signal(barrier, inc=1, device_id={"dp": me + 1}, device_id_type=MESH)

    @pl.when(me > 0)
    def _():
        pl.semaphore_signal(barrier, inc=1, device_id={"dp": me - 1}, device_id_type=MESH)

    pl.semaphore_signal(barrier, inc=1, device_id={"parts": 1 - part}, device_id_type=MESH)
    pl.semaphore_signal(barrier, inc=1, device_id={"rep": 1 - rep}, device_id_type=MESH)
    for k in range(1, mps):
        pl.semaphore_signal(barrier, inc=1, device_id={"mp": other(k)}, device_id_type=MESH)

    inner = (me > 0) & (me < n - 1)

    @pl.when(inner)
    def _():
        pl.semaphore_wait(barrier, 3 + mps)

    @pl.when(jnp.logical_not(inner))
    def _():
        pl.semaphore_wait(barrier, 2 + mps)

    own(0)
    own(1)
    steps(0, 1, n - 1)
    own(2)
    steps(0, n - 1, n)
    finish(0)

    lanes = lax.broadcasted_iota(jnp.int32, (1, LANES), 1) < HEAD
    keys_at = lax.broadcasted_iota(jnp.int32, (1, seq), 1)
    cuts = [1 + (n - 1) * k // 3 for k in range(4)]

    def attend(doc, carry):
        normed = normed_rows(hid_ref[doc].astype(jnp.float32))
        proj[...] = jnp.dot(normed, q_buf[...], preferred_element_type=jnp.float32).astype(jnp.bfloat16)
        visible = keys_at < len_ref[doc]

        for pair in range(heads_wide // LANES):
            queries = proj[:, pair * LANES:(pair + 1) * LANES]
            keys = proj[:, heads_wide + pair * LANES:heads_wide + (pair + 1) * LANES]
            values = proj[:, 2 * heads_wide + pair * LANES:2 * heads_wide + (pair + 1) * LANES]
            queries = queries * jnp.asarray(HEAD ** (-0.5), jnp.bfloat16)
            blank = jnp.zeros_like(queries)
            made = []
            for mine in (lanes, jnp.logical_not(lanes)):
                scores = lax.dot_general(
                    jnp.where(mine, queries, blank), keys, (((1,), (1,)), ((), ())),
                    preferred_element_type=jnp.float32,
                )
                scores = jnp.where(visible, scores, -jnp.inf)
                weights = jnp.exp(scores - jnp.max(scores, axis=1, keepdims=True))
                total = jnp.sum(weights, axis=1, keepdims=True)
                weights = (weights * (1.0 / total)).astype(jnp.bfloat16)
                made.append(jnp.dot(weights, values, preferred_element_type=jnp.float32))
            context = jnp.where(lanes, made[0], made[1]).astype(jnp.bfloat16)
            c_buf[my_mp, doc, :, pair * LANES:(pair + 1) * LANES] = context

        for k in range(1, mps):
            context_copy(my_mp, k, doc).start()

        @pl.when(doc == 0)
        def _():
            steps(1, 1, n)
            finish(1)
            for k in range(1, mps):
                out_copy(my_mp, k).start()

        for k in range(3):
            @pl.when(doc == min(k + 1, docs - 1))
            def _():
                steps(2, cuts[k], cuts[k + 1])

        return carry

    lax.fori_loop(0, docs, attend, 0)
    for k in range(1, mps):
        out_copy(other(k), k).wait_recv()
        out_beside(other(k), rep).start()
    finish(2)
    for k in range(1, mps):
        out_beside(other(k), 1 - rep).wait_recv()

    def feed(doc, carry):
        for k in range(1, mps):
            context_copy(other(k), k, doc).wait_recv()
        residual = hid_ref[doc].astype(jnp.float32)
        for owner in range(mps):
            context = c_buf[owner, doc]
            product = jnp.concatenate(
                [jnp.dot(context, o_buf[owner, j], preferred_element_type=jnp.float32) for j in range(n)], axis=1
            )
            residual = residual + product.astype(jnp.bfloat16).astype(jnp.float32)
        valid = lax.broadcasted_iota(jnp.int32, (seq, 1), 0) < len_ref[doc]
        res_ref[doc] = jnp.sum(jnp.where(valid, residual, 0.0), axis=0, keepdims=True)
        normed = normed_rows(residual)
        wide = u_buf.shape[1]
        block = wide // 4
        for k in range(4):
            hidden = jnp.dot(normed, u_buf[:, k * block:(k + 1) * block], preferred_element_type=jnp.float32)
            hidden = 0.5 * hidden * (1.0 + lax.erf(hidden * (0.5 ** 0.5)))
            hidden = hidden.astype(jnp.bfloat16).astype(jnp.float32)
            act_ref[doc, :, k * block:(k + 1) * block] = jnp.sum(
                jnp.where(valid, hidden, 0.0), axis=0, keepdims=True
            )
        return carry

    lax.fori_loop(0, docs, feed, 0)

    for which in range(3):
        sent(which)

    def unsent(doc, carry):
        for k in range(1, mps):
            context_copy(my_mp, k, doc).wait_send()
        return carry

    lax.fori_loop(0, docs, unsent, 0)
    for k in range(1, mps):
        out_copy(my_mp, k).wait_send()
        out_beside(other(k), rep).wait_send()


def encode(lengths, hidden, w_qkv, w_out, w_up):
    n, mps = lax.axis_size("dp"), lax.axis_size("mp")
    docs, seq, width = hidden.shape
    splits = tuple(
        4 if extent % (4 * unit) == 0 else 2
        for extent, unit in ((w_qkv.shape[1], LANES), (w_out.shape[0], 16), (w_up.shape[1], LANES))
    )
    heads_wide = w_qkv.shape[1] // 3
    whole = pl.BlockSpec(memory_space=pltpu.VMEM)
    dma = pltpu.SemaphoreType.DMA
    return pl.pallas_call(
        functools.partial(encode_kernel, n, mps, splits),
        out_shape=(
            jax.ShapeDtypeStruct((docs, 1, w_up.shape[1]), jnp.float32),
            jax.ShapeDtypeStruct((docs, 1, width), jnp.float32),
        ),
        in_specs=[pl.BlockSpec(memory_space=pltpu.SMEM)] + [whole] * 4,
        out_specs=(whole, whole),
        scratch_shapes=[
            pltpu.VMEM((width, w_qkv.shape[1]), jnp.bfloat16),
            pltpu.VMEM((mps, n) + w_out.shape, jnp.bfloat16),
            pltpu.VMEM((width, w_up.shape[1]), jnp.bfloat16),
            pltpu.VMEM((mps, docs, seq, heads_wide), jnp.bfloat16),
            pltpu.VMEM((seq, w_qkv.shape[1]), jnp.bfloat16),
            dma((3, n, 5)),
            dma((3, n, 4)),
            dma((mps, docs)),
            dma((mps, docs)),
            dma((mps,)),
            dma((mps,)),
            dma((mps,)),
            dma((mps,)),
        ],
        compiler_params=pltpu.CompilerParams(
            collective_id=0, has_side_effects=True, vmem_limit_bytes=52 * 1024 * 1024
        ),
        cost_estimate=pl.CostEstimate(flops=12 * 10**9, bytes_accessed=10**8, transcendentals=10**6),
    )(lengths, hidden, w_qkv, w_out, w_up)


def pool_kernel(
    n, mps, reps, act_ref, res_ref, w_ref, key_ref, out_ref, keys_ref,
    a_buf, r_buf, a_send, a_recv, r_send, r_recv, p_send, p_recv, k_send, k_recv,
):
    me, my_mp, rep = lax.axis_index("dp"), lax.axis_index("mp"), lax.axis_index("rep")
    count = n * mps * reps
    place = (me * mps + my_mp) * reps + rep

    def at(number):
        return {"dp": number // (mps * reps), "mp": number // reps % mps, "rep": number % reps}

    barrier = pltpu.get_barrier_semaphore()

    def greet(k, carry):
        pl.semaphore_signal(barrier, inc=1, device_id=at(lax.rem(place + k, count)), device_id_type=MESH)
        return carry

    lax.fori_loop(1, count, greet, 0)
    pl.semaphore_wait(barrier, count - 1)

    def act_copy(source, target):
        return pltpu.make_async_remote_copy(
            src_ref=act_ref, dst_ref=a_buf.at[source], send_sem=a_send.at[target], recv_sem=a_recv.at[source],
            device_id={"dp": target}, device_id_type=MESH,
        )

    def res_copy(source, target):
        return pltpu.make_async_remote_copy(
            src_ref=res_ref.at[target], dst_ref=r_buf.at[source], send_sem=r_send.at[target],
            recv_sem=r_recv.at[source], device_id={"dp": target}, device_id_type=MESH,
        )

    def give(k, carry):
        target = lax.rem(me + k, n)
        act_copy(me, target).start()
        res_copy(me, target).start()
        return carry

    lax.fori_loop(1, n, give, 0)

    def key_copy(source, target):
        return pltpu.make_async_remote_copy(
            src_ref=keys_ref.at[source], dst_ref=keys_ref.at[source], send_sem=k_send.at[target],
            recv_sem=k_recv.at[source], device_id=at(target), device_id_type=MESH,
        )

    keys_ref[place] = key_ref[...]

    def tell(k, carry):
        key_copy(place, lax.rem(place + k, count)).start()
        return carry

    lax.fori_loop(1, count, tell, 0)
    a_buf[me] = act_ref[...]
    r_buf[me] = res_ref[me]

    def take(k, carry):
        source = lax.rem(me + k, n)
        act_copy(source, source).wait()
        res_copy(source, source).wait()
        return carry

    lax.fori_loop(1, n, take, 0)
    acts = jnp.concatenate([a_buf[j] for j in range(n)], axis=0)
    high = acts.astype(jnp.bfloat16)
    low = (acts - high.astype(jnp.float32)).astype(jnp.bfloat16)
    part = jnp.dot(high, w_ref[...], preferred_element_type=jnp.float32)
    part = part + jnp.dot(low, w_ref[...], preferred_element_type=jnp.float32)
    rest = jnp.concatenate([r_buf[j] for j in range(n)], axis=0)
    out_ref[place] = part + jnp.where(my_mp == 0, 1.0, 0.0) * rest

    def part_copy(source, target):
        return pltpu.make_async_remote_copy(
            src_ref=out_ref.at[source], dst_ref=out_ref.at[source], send_sem=p_send.at[target],
            recv_sem=p_recv.at[source], device_id=at(target), device_id_type=MESH,
        )

    def share(k, carry):
        part_copy(place, lax.rem(place + k, count)).start()
        return carry

    lax.fori_loop(1, count, share, 0)

    def collect(k, carry):
        source = lax.rem(place + k, count)
        part_copy(source, source).wait()
        key_copy(source, source).wait()
        return carry

    lax.fori_loop(1, count, collect, 0)


def pool(acts, rest, w_down, key):
    n, mps, reps = lax.axis_size("dp"), lax.axis_size("mp"), lax.axis_size("rep")
    docs = acts.shape[0]
    count = n * mps * reps
    whole = pl.BlockSpec(memory_space=pltpu.VMEM)
    dma = pltpu.SemaphoreType.DMA
    return pl.pallas_call(
        functools.partial(pool_kernel, n, mps, reps),
        out_shape=(
            jax.ShapeDtypeStruct((count, n * docs, w_down.shape[1]), jnp.float32),
            jax.ShapeDtypeStruct((count,) + key.shape, jnp.int32),
        ),
        in_specs=[whole] * 4,
        out_specs=(whole, whole),
        scratch_shapes=[
            pltpu.VMEM((n,) + acts.shape, jnp.float32),
            pltpu.VMEM(rest.shape, jnp.float32),
            dma((n,)), dma((n,)), dma((n,)), dma((n,)), dma((count,)), dma((count,)), dma((count,)), dma((count,)),
        ],
        compiler_params=pltpu.CompilerParams(
            collective_id=1, has_side_effects=True, vmem_limit_bytes=52 * 1024 * 1024
        ),
    )(acts, rest, w_down, key)


def shards(hidden_in, doc_lengths, w_qkv, w_out, w_up, w_down, stored_embed, doc_labels, doc_order):
    n, mps, reps = lax.axis_size("dp"), lax.axis_size("mp"), lax.axis_size("rep")
    docs, _, width = hidden_in.shape
    place = (lax.axis_index("dp") * mps + lax.axis_index("mp")) * reps + lax.axis_index("rep")
    blocks = n * mps * reps
    rows = doc_order.shape[0]
    new_count = docs // mps
    ranks = blocks * rows

    stored_units = unit_rows(stored_embed.astype(jnp.float32))
    labels = doc_labels[:, 0]
    own_key = labels * ranks + doc_order
    spare = -stored_units.shape[0] % 16
    all_stored = lax.all_gather(
        jnp.pad(stored_units, ((0, spare), (0, 0))), ("dp", "mp", "rep"), axis=0, tiled=True
    )

    acts, rest = encode(doc_lengths, hidden_in, w_qkv.reshape(w_qkv.shape[0], -1), w_out, w_up)
    scale = 1.0 / doc_lengths[:, None].astype(jnp.float32)
    acts = acts[:, 0] * scale
    rest = (rest[:, 0] * scale).reshape(docs, n, width // n).transpose(1, 0, 2)
    sent_key = jnp.pad(own_key, (0, -rows % LANES))[None]
    parts, keys = pool(acts, rest, w_down, sent_key)
    keys = keys[:, 0, :rows]
    stored_keys = jnp.pad(keys[:, new_count:], ((0, 0), (0, spare)), constant_values=-1)
    pooled = jnp.sum(parts.reshape(n, mps, reps, n, docs, width // n), axis=1)
    pooled = pooled.transpose(2, 1, 3, 0, 4).reshape(n, reps, mps, new_count, width)
    new_units = unit_rows(pooled).transpose(0, 2, 1, 3, 4).reshape(blocks * new_count, width)
    own_new = lax.dynamic_slice_in_dim(new_units, place * new_count, new_count, 0)
    own_rows = jnp.concatenate([own_new, stored_units], axis=0)

    def best_of(units, unit_keys):
        similar = lax.dot_general(
            own_rows, units, (((1,), (1,)), ((), ())), preferred_element_type=jnp.float32
        )
        unit_keys = unit_keys.reshape(1, -1)
        earlier = (unit_keys < own_key[:, None]) & (unit_keys >= (labels * ranks)[:, None])
        return jnp.max(jnp.where(earlier, similar, -2.0), axis=1)

    largest = jnp.maximum(best_of(all_stored, stored_keys), best_of(new_units, keys[:, :new_count]))
    return jnp.where(largest < -1.5, 0.0, largest)


def solution(mesh):
    placed = (
        P(("parts", "dp", "rep"), None, None),
        P(("parts", "dp", "rep")),
        P("dp", None, "mp"),
        P("mp", "dp"),
        P("dp", "mp"),
        P("mp", "dp"),
        P(("parts", "dp", "mp", "rep"), None),
        P(("parts", "dp", "mp", "rep"), None),
        P(("parts", "dp", "mp", "rep")),
    )
    return jax.shard_map(
        shards,
        mesh=mesh,
        in_specs=placed,
        out_specs=P(("parts", "dp", "mp", "rep")),
        check_vma=False,
    )
```

```python
import functools

import jax
import jax.numpy as jnp
from jax import lax
from jax.experimental import pallas as pl
from jax.experimental.pallas import tpu as pltpu
from jax.sharding import PartitionSpec as P

HEAD = 64
LANES = 128
MESH = pl.DeviceIdType.MESH


def unit_rows(values):
    return (values * lax.rsqrt(jnp.sum(values * values, axis=-1, keepdims=True) + 1e-06)).astype(
        jnp.bfloat16
    )


def normed_rows(values):
    centred = values - jnp.mean(values, axis=-1, keepdims=True)
    spread = jnp.mean(centred * centred, axis=-1, keepdims=True)
    return (centred * lax.rsqrt(spread + 1e-05)).astype(jnp.bfloat16)


def encode_kernel(
    n, mps, splits, len_ref, hid_ref, wq_ref, wo_ref, wu_ref, act_ref, res_ref,
    q_buf, o_buf, u_buf, c_buf, proj, z_send, z_recv, c_send, c_recv, x_send, x_recv, y_send, y_recv,
):
    me, my_mp = lax.axis_index("dp"), lax.axis_index("mp")
    part, rep = lax.axis_index("parts"), lax.axis_index("rep")
    docs, seq, _ = hid_ref.shape
    heads_wide = c_buf.shape[3]
    depth = wq_ref.shape[0]
    out_rows = wo_ref.shape[0]

    def piece(which, source, p, r):
        number = splits[which]
        group = p * 2 + r if number == 4 else p
        if which == 1:
            rows = out_rows // number
            return o_buf.at[my_mp, source, pl.ds(pl.multiple_of(group * rows, 16), rows), :]
        buf = q_buf if which == 0 else u_buf
        wide = buf.shape[1] // number
        return buf.at[
            pl.ds(pl.multiple_of(source * depth, 16), depth),
            pl.ds(pl.multiple_of(group * wide, LANES), wide),
        ]

    def copy_of(which, source, p, r, send, recv, device):
        ref = piece(which, source, p, r)
        return pltpu.make_async_remote_copy(
            src_ref=ref, dst_ref=ref, send_sem=z_send.at[which, source, send],
            recv_sem=z_recv.at[which, source, recv], device_id=device, device_id_type=MESH,
        )

    def right(which, source):
        return copy_of(which, source, part, rep, 0, 0, {"dp": me + 1})

    def left(which, source):
        return copy_of(which, source, part, rep, 4, 0, {"dp": me - 1})

    def across(which, source, p):
        return copy_of(which, source, p, rep, 1, 1, {"parts": 1 - part})

    def beside(which, source, r):
        return copy_of(which, source, part, r, 2, 2, {"rep": 1 - rep})

    def beside_late(which, source, p, r):
        return copy_of(which, source, p, r, 3, 3, {"rep": 1 - rep})

    def own(which):
        @pl.when(me < n - 1)
        def _():
            right(which, me).start()

        @pl.when(me > 0)
        def _():
            left(which, me).start()

    def on_z(which, source, rightward):
        way = right if rightward else left
        way(which, source).wait_recv()

        @pl.when(me < n - 1 if rightward else me > 0)
        def _():
            way(which, source).start()

        across(which, source, part).start()
        if splits[which] == 4:
            beside(which, source, rep).start()

    def on_y(which, source):
        across(which, source, 1 - part).wait_recv()
        if splits[which] == 4:
            beside_late(which, source, 1 - part, rep).start()

    def both(step, fn):
        @pl.when(step <= me)
        def _():
            fn(me - step, True)

        @pl.when(me + step <= n - 1)
        def _():
            fn(me + step, False)

    def steps(which, lo, hi):
        def body(step, carry):
            both(step, lambda source, way: on_z(which, source, way))

            @pl.when(step > 1)
            def _():
                both(step - 1, lambda source, way: on_y(which, source))

            return carry

        lax.fori_loop(lo, hi, body, 0)

    def finish(which):
        both(n - 1, lambda source, way: on_y(which, source))
        if splits[which] == 4:

            def body(step, carry):
                def take(source, way):
                    beside(which, source, 1 - rep).wait_recv()
                    beside_late(which, source, 1 - part, 1 - rep).wait_recv()

                both(step, take)
                return carry

            lax.fori_loop(1, n, body, 0)

    def sent(which):
        @pl.when(me < n - 1)
        def _():
            right(which, me).wait_send()

        @pl.when(me > 0)
        def _():
            left(which, me).wait_send()

        def body(step, carry):
            def drop(source, way):
                @pl.when(me < n - 1 if way else me > 0)
                def _():
                    (right if way else left)(which, source).wait_send()

                across(which, source, part).wait_send()
                if splits[which] == 4:
                    beside(which, source, rep).wait_send()
                    beside_late(which, source, 1 - part, rep).wait_send()

            both(step, drop)
            return carry

        lax.fori_loop(1, n, body, 0)

    def other(k):
        return lax.rem(my_mp + k, mps)

    def context_copy(owner, k, doc):
        ref = c_buf.at[owner, doc]
        return pltpu.make_async_remote_copy(
            src_ref=ref, dst_ref=ref, send_sem=c_send.at[k, doc], recv_sem=c_recv.at[owner, doc],
            device_id={"mp": other(k)}, device_id_type=MESH,
        )

    half = out_rows // 2

    def out_half(owner, r):
        return o_buf.at[owner, :, pl.ds(pl.multiple_of(r * half, 16), half), :]

    def out_copy(owner, k):
        ref = out_half(owner, rep)
        return pltpu.make_async_remote_copy(
            src_ref=ref, dst_ref=ref, send_sem=x_send.at[k], recv_sem=x_recv.at[owner],
            device_id={"mp": other(k)}, device_id_type=MESH,
        )

    def out_beside(owner, r):
        ref = out_half(owner, r)
        return pltpu.make_async_remote_copy(
            src_ref=ref, dst_ref=ref, send_sem=y_send.at[owner], recv_sem=y_recv.at[owner],
            device_id={"rep": 1 - rep}, device_id_type=MESH,
        )

    q_buf[pl.ds(pl.multiple_of(me * depth, 16), depth), :] = wq_ref[...]
    o_buf[my_mp, me] = wo_ref[...]
    u_buf[pl.ds(pl.multiple_of(me * depth, 16), depth), :] = wu_ref[...]

    barrier = pltpu.get_barrier_semaphore()

    @pl.when(me < n - 1)
    def _():
        pl.semaphore_signal(barrier, inc=1, device_id={"dp": me + 1}, device_id_type=MESH)

    @pl.when(me > 0)
    def _():
        pl.semaphore_signal(barrier, inc=1, device_id={"dp": me - 1}, device_id_type=MESH)

    pl.semaphore_signal(barrier, inc=1, device_id={"parts": 1 - part}, device_id_type=MESH)
    pl.semaphore_signal(barrier, inc=1, device_id={"rep": 1 - rep}, device_id_type=MESH)
    for k in range(1, mps):
        pl.semaphore_signal(barrier, inc=1, device_id={"mp": other(k)}, device_id_type=MESH)

    inner = (me > 0) & (me < n - 1)

    @pl.when(inner)
    def _():
        pl.semaphore_wait(barrier, 3 + mps)

    @pl.when(jnp.logical_not(inner))
    def _():
        pl.semaphore_wait(barrier, 2 + mps)

    own(1)
    own(0)
    steps(1, 1, n)
    finish(1)
    for k in range(1, mps):
        out_copy(my_mp, k).start()
    steps(0, 1, n - 1)
    own(2)
    steps(0, n - 1, n)
    finish(0)

    lanes = lax.broadcasted_iota(jnp.int32, (1, LANES), 1) < HEAD
    keys_at = lax.broadcasted_iota(jnp.int32, (1, seq), 1)
    cuts = [1 + (n - 1) * k // 3 for k in range(4)]

    def attend(doc, carry):
        normed = normed_rows(hid_ref[doc].astype(jnp.float32))
        proj[...] = jnp.dot(normed, q_buf[...], preferred_element_type=jnp.float32).astype(jnp.bfloat16)
        visible = keys_at < len_ref[doc]

        for pair in range(heads_wide // LANES):
            queries = proj[:, pair * LANES:(pair + 1) * LANES]
            keys = proj[:, heads_wide + pair * LANES:heads_wide + (pair + 1) * LANES]
            values = proj[:, 2 * heads_wide + pair * LANES:2 * heads_wide + (pair + 1) * LANES]
            queries = queries * jnp.asarray(HEAD ** (-0.5), jnp.bfloat16)
            blank = jnp.zeros_like(queries)
            made = []
            for mine in (lanes, jnp.logical_not(lanes)):
                scores = lax.dot_general(
                    jnp.where(mine, queries, blank), keys, (((1,), (1,)), ((), ())),
                    preferred_element_type=jnp.float32,
                )
                scores = jnp.where(visible, scores, -jnp.inf)
                weights = jnp.exp(scores - jnp.max(scores, axis=1, keepdims=True))
                total = jnp.sum(weights, axis=1, keepdims=True)
                weights = (weights * (1.0 / total)).astype(jnp.bfloat16)
                made.append(jnp.dot(weights, values, preferred_element_type=jnp.float32))
            context = jnp.where(lanes, made[0], made[1]).astype(jnp.bfloat16)
            c_buf[my_mp, doc, :, pair * LANES:(pair + 1) * LANES] = context

        for k in range(1, mps):
            context_copy(my_mp, k, doc).start()

        for k in range(3):
            @pl.when(doc == min(k + 1, docs - 1))
            def _():
                steps(2, cuts[k], cuts[k + 1])

        return carry

    lax.fori_loop(0, docs, attend, 0)
    for k in range(1, mps):
        out_copy(other(k), k).wait_recv()
        out_beside(other(k), rep).start()
    finish(2)
    for k in range(1, mps):
        out_beside(other(k), 1 - rep).wait_recv()

    def feed(doc, carry):
        for k in range(1, mps):
            context_copy(other(k), k, doc).wait_recv()
        residual = hid_ref[doc].astype(jnp.float32)
        for owner in range(mps):
            context = c_buf[owner, doc]
            product = jnp.concatenate(
                [jnp.dot(context, o_buf[owner, j], preferred_element_type=jnp.float32) for j in range(n)], axis=1
            )
            residual = residual + product.astype(jnp.bfloat16).astype(jnp.float32)
        valid = lax.broadcasted_iota(jnp.int32, (seq, 1), 0) < len_ref[doc]
        res_ref[doc] = jnp.sum(jnp.where(valid, residual, 0.0), axis=0, keepdims=True)
        normed = normed_rows(residual)
        wide = u_buf.shape[1]
        block = wide // 4
        for k in range(4):
            hidden = jnp.dot(normed, u_buf[:, k * block:(k + 1) * block], preferred_element_type=jnp.float32)
            hidden = 0.5 * hidden * (1.0 + lax.erf(hidden * (0.5 ** 0.5)))
            hidden = hidden.astype(jnp.bfloat16).astype(jnp.float32)
            act_ref[doc, :, k * block:(k + 1) * block] = jnp.sum(
                jnp.where(valid, hidden, 0.0), axis=0, keepdims=True
            )
        return carry

    lax.fori_loop(0, docs, feed, 0)

    for which in range(3):
        sent(which)

    def unsent(doc, carry):
        for k in range(1, mps):
            context_copy(my_mp, k, doc).wait_send()
        return carry

    lax.fori_loop(0, docs, unsent, 0)
    for k in range(1, mps):
        out_copy(my_mp, k).wait_send()
        out_beside(other(k), rep).wait_send()


def encode(lengths, hidden, w_qkv, w_out, w_up):
    n, mps = lax.axis_size("dp"), lax.axis_size("mp")
    docs, seq, width = hidden.shape
    splits = tuple(
        4 if extent % (4 * unit) == 0 else 2
        for extent, unit in ((w_qkv.shape[1], LANES), (w_out.shape[0], 16), (w_up.shape[1], LANES))
    )
    heads_wide = w_qkv.shape[1] // 3
    whole = pl.BlockSpec(memory_space=pltpu.VMEM)
    dma = pltpu.SemaphoreType.DMA
    return pl.pallas_call(
        functools.partial(encode_kernel, n, mps, splits),
        out_shape=(
            jax.ShapeDtypeStruct((docs, 1, w_up.shape[1]), jnp.float32),
            jax.ShapeDtypeStruct((docs, 1, width), jnp.float32),
        ),
        in_specs=[pl.BlockSpec(memory_space=pltpu.SMEM)] + [whole] * 4,
        out_specs=(whole, whole),
        scratch_shapes=[
            pltpu.VMEM((width, w_qkv.shape[1]), jnp.bfloat16),
            pltpu.VMEM((mps, n) + w_out.shape, jnp.bfloat16),
            pltpu.VMEM((width, w_up.shape[1]), jnp.bfloat16),
            pltpu.VMEM((mps, docs, seq, heads_wide), jnp.bfloat16),
            pltpu.VMEM((seq, w_qkv.shape[1]), jnp.bfloat16),
            dma((3, n, 5)),
            dma((3, n, 4)),
            dma((mps, docs)),
            dma((mps, docs)),
            dma((mps,)),
            dma((mps,)),
            dma((mps,)),
            dma((mps,)),
        ],
        compiler_params=pltpu.CompilerParams(
            collective_id=0, has_side_effects=True, vmem_limit_bytes=52 * 1024 * 1024
        ),
        cost_estimate=pl.CostEstimate(flops=12 * 10**9, bytes_accessed=10**8, transcendentals=10**6),
    )(lengths, hidden, w_qkv, w_out, w_up)


def pool_kernel(
    n, mps, reps, act_ref, res_ref, w_ref, key_ref, out_ref, keys_ref,
    a_buf, r_buf, a_send, a_recv, r_send, r_recv, p_send, p_recv, k_send, k_recv,
):
    me, my_mp, rep = lax.axis_index("dp"), lax.axis_index("mp"), lax.axis_index("rep")
    count = n * mps * reps
    place = (me * mps + my_mp) * reps + rep

    def at(number):
        return {"dp": number // (mps * reps), "mp": number // reps % mps, "rep": number % reps}

    barrier = pltpu.get_barrier_semaphore()

    def greet(k, carry):
        pl.semaphore_signal(barrier, inc=1, device_id=at(lax.rem(place + k, count)), device_id_type=MESH)
        return carry

    lax.fori_loop(1, count, greet, 0)
    pl.semaphore_wait(barrier, count - 1)

    def act_copy(source, target):
        return pltpu.make_async_remote_copy(
            src_ref=act_ref, dst_ref=a_buf.at[source], send_sem=a_send.at[target], recv_sem=a_recv.at[source],
            device_id={"dp": target}, device_id_type=MESH,
        )

    def res_copy(source, target):
        return pltpu.make_async_remote_copy(
            src_ref=res_ref.at[target], dst_ref=r_buf.at[source], send_sem=r_send.at[target],
            recv_sem=r_recv.at[source], device_id={"dp": target}, device_id_type=MESH,
        )

    def give(k, carry):
        target = lax.rem(me + k, n)
        act_copy(me, target).start()
        res_copy(me, target).start()
        return carry

    lax.fori_loop(1, n, give, 0)

    def key_copy(source, target):
        return pltpu.make_async_remote_copy(
            src_ref=keys_ref.at[source], dst_ref=keys_ref.at[source], send_sem=k_send.at[target],
            recv_sem=k_recv.at[source], device_id=at(target), device_id_type=MESH,
        )

    keys_ref[place] = key_ref[...]

    def tell(k, carry):
        key_copy(place, lax.rem(place + k, count)).start()
        return carry

    lax.fori_loop(1, count, tell, 0)
    a_buf[me] = act_ref[...]
    r_buf[me] = res_ref[me]

    def take(k, carry):
        source = lax.rem(me + k, n)
        act_copy(source, source).wait()
        res_copy(source, source).wait()
        return carry

    lax.fori_loop(1, n, take, 0)
    acts = jnp.concatenate([a_buf[j] for j in range(n)], axis=0)
    high = acts.astype(jnp.bfloat16)
    low = (acts - high.astype(jnp.float32)).astype(jnp.bfloat16)
    part = jnp.dot(high, w_ref[...], preferred_element_type=jnp.float32)
    part = part + jnp.dot(low, w_ref[...], preferred_element_type=jnp.float32)
    rest = jnp.concatenate([r_buf[j] for j in range(n)], axis=0)
    out_ref[place] = part + jnp.where(my_mp == 0, 1.0, 0.0) * rest

    def part_copy(source, target):
        return pltpu.make_async_remote_copy(
            src_ref=out_ref.at[source], dst_ref=out_ref.at[source], send_sem=p_send.at[target],
            recv_sem=p_recv.at[source], device_id=at(target), device_id_type=MESH,
        )

    def share(k, carry):
        part_copy(place, lax.rem(place + k, count)).start()
        return carry

    lax.fori_loop(1, count, share, 0)

    def collect(k, carry):
        source = lax.rem(place + k, count)
        part_copy(source, source).wait()
        key_copy(source, source).wait()
        return carry

    lax.fori_loop(1, count, collect, 0)


def pool(acts, rest, w_down, key):
    n, mps, reps = lax.axis_size("dp"), lax.axis_size("mp"), lax.axis_size("rep")
    docs = acts.shape[0]
    count = n * mps * reps
    whole = pl.BlockSpec(memory_space=pltpu.VMEM)
    dma = pltpu.SemaphoreType.DMA
    return pl.pallas_call(
        functools.partial(pool_kernel, n, mps, reps),
        out_shape=(
            jax.ShapeDtypeStruct((count, n * docs, w_down.shape[1]), jnp.float32),
            jax.ShapeDtypeStruct((count,) + key.shape, jnp.int32),
        ),
        in_specs=[whole] * 4,
        out_specs=(whole, whole),
        scratch_shapes=[
            pltpu.VMEM((n,) + acts.shape, jnp.float32),
            pltpu.VMEM(rest.shape, jnp.float32),
            dma((n,)), dma((n,)), dma((n,)), dma((n,)), dma((count,)), dma((count,)), dma((count,)), dma((count,)),
        ],
        compiler_params=pltpu.CompilerParams(
            collective_id=1, has_side_effects=True, vmem_limit_bytes=52 * 1024 * 1024
        ),
    )(acts, rest, w_down, key)


def shards(hidden_in, doc_lengths, w_qkv, w_out, w_up, w_down, stored_embed, doc_labels, doc_order):
    n, mps, reps = lax.axis_size("dp"), lax.axis_size("mp"), lax.axis_size("rep")
    docs, _, width = hidden_in.shape
    place = (lax.axis_index("dp") * mps + lax.axis_index("mp")) * reps + lax.axis_index("rep")
    blocks = n * mps * reps
    rows = doc_order.shape[0]
    new_count = docs // mps
    ranks = blocks * rows

    stored_units = unit_rows(stored_embed.astype(jnp.float32))
    labels = doc_labels[:, 0]
    own_key = labels * ranks + doc_order
    spare = -stored_units.shape[0] % 16
    all_stored = lax.all_gather(
        jnp.pad(stored_units, ((0, spare), (0, 0))), ("dp", "mp", "rep"), axis=0, tiled=True
    )

    acts, rest = encode(doc_lengths, hidden_in, w_qkv.reshape(w_qkv.shape[0], -1), w_out, w_up)
    scale = 1.0 / doc_lengths[:, None].astype(jnp.float32)
    acts = acts[:, 0] * scale
    rest = (rest[:, 0] * scale).reshape(docs, n, width // n).transpose(1, 0, 2)
    sent_key = jnp.pad(own_key, (0, -rows % LANES))[None]
    parts, keys = pool(acts, rest, w_down, sent_key)
    keys = keys[:, 0, :rows]
    stored_keys = jnp.pad(keys[:, new_count:], ((0, 0), (0, spare)), constant_values=-1)
    pooled = jnp.sum(parts.reshape(n, mps, reps, n, docs, width // n), axis=1)
    pooled = pooled.transpose(2, 1, 3, 0, 4).reshape(n, reps, mps, new_count, width)
    new_units = unit_rows(pooled).transpose(0, 2, 1, 3, 4).reshape(blocks * new_count, width)
    own_new = lax.dynamic_slice_in_dim(new_units, place * new_count, new_count, 0)
    own_rows = jnp.concatenate([own_new, stored_units], axis=0)

    def best_of(units, unit_keys):
        similar = lax.dot_general(
            own_rows, units, (((1,), (1,)), ((), ())), preferred_element_type=jnp.float32
        )
        unit_keys = unit_keys.reshape(1, -1)
        earlier = (unit_keys < own_key[:, None]) & (unit_keys >= (labels * ranks)[:, None])
        return jnp.max(jnp.where(earlier, similar, -2.0), axis=1)

    largest = jnp.maximum(best_of(all_stored, stored_keys), best_of(new_units, keys[:, :new_count]))
    return jnp.where(largest < -1.5, 0.0, largest)


def solution(mesh):
    placed = (
        P(("parts", "dp", "rep"), None, None),
        P(("parts", "dp", "rep")),
        P("dp", None, "mp"),
        P("mp", "dp"),
        P("dp", "mp"),
        P("mp", "dp"),
        P(("parts", "dp", "mp", "rep"), None),
        P(("parts", "dp", "mp", "rep"), None),
        P(("parts", "dp", "mp", "rep")),
    )
    return jax.shard_map(
        shards,
        mesh=mesh,
        in_specs=placed,
        out_specs=P(("parts", "dp", "mp", "rep")),
        check_vma=False,
    )
```
